32 devices in a mesh: row: 8 (over z, y), col: 4 (over x, core).
Axes of the slice: x: 2, y: 2, z: 4, core: 2. Of those that a mesh axis runs over, the one named last changes fastest.
Arguments:
- object_field: float32 [2, 3072, 1024], P(None, 'row', 'col'), may hold values from -3 to 3
- probe_field: float32 [2, 256, 256], replicated, may hold values from -6 to 6
- amplitudes: bfloat16 [8, 4, 4, 256, 256], P('row', 'col'), may hold values from 0.5 to 16
- pos_rows: int32 [8, 4, 4], P('row', 'col'), may hold values from 0 to 383
- pos_cols: int32 [8, 4, 4], P('row', 'col'), may hold values from 0 to 255
- scan_pick: int32 [8, 4, 2], P('row', 'col'), may hold values from 0 to 3
- scan_count: int32 [32], P(('row', 'col')), may hold values from 1 to 2, 48 in all
Outputs:
- object_next: float32 [2, 3072, 1024], P(None, 'row', 'col')
- probe_next: float32 [2, 256, 256], replicated
The draws below stay inside these ranges and needn't reach their ends.
Inputs may be any that keep to these rules, and one draw needn't show every extreme that they name: `scan_count`: each tile's list has 1 to 2 scans; the longest list has exactly 2; lists total 48 scans.
All inputs are finite; a program needn't handle non-finite values. No bound on the sum of `scan_count` on one device may be relied on, other than what follows from the above.
Results may differ from the reference program's by a relative error of at most 0.0003.
Values sent between devices are 32-bit elements; how exact they have to be, the bound alone decides.
A program may use at most 64 MiB of HBM per device.

```python
import math
import jax
import jax.numpy as jnp
import numpy as np
from jax import lax

PW = 256
TH = 384
TW = 256
SCAP = 2
POOL = 4
NH = 3072
NW = 1024
TILES = 32
USED = 48
N_ROW = 8
N_COL = 4


def touch_ends(array, stream_key, smallest, largest):
    shape = array.shape
    index_at = [jax.random.randint(jax.random.fold_in(stream_key, axis), (), 0, shape[axis]) for axis in range(len(shape))]
    array = array.at[tuple(index_at)].set(smallest)
    longest = shape.index(max(shape))
    index_at[longest] = (index_at[longest] + 1) % shape[longest]
    return array.at[tuple(index_at)].set(largest)


def block_scale(key, dims, shards, low, largest):
    loudness = 1.0
    for position, parts in shards:
        heights = jax.random.uniform(jax.random.fold_in(jax.random.fold_in(key, 6), position), (parts,), jnp.float32, low / len(shards), largest / len(shards))
        loudness = loudness * jnp.repeat(jnp.exp(heights), dims[position] // parts).reshape((-1,) + (1,) * (len(dims) - 1 - position))
    return loudness


def length_profile(amount, total, bound, lean):
    weights = [(1 << 20) // math.isqrt(rank ** lean) + 1 for rank in range(2, amount + 1)]
    rest, counts = total - bound - (amount - 1), [1] * (amount - 1)
    while rest > 0:
        free = [i for i in range(amount - 1) if counts[i] < bound]
        whole, budget = sum([weights[i] for i in free]), rest
        for i in free:
            extra = min(bound - counts[i], max(1, budget * weights[i] // whole), rest)
            counts[i] = counts[i] + extra
            rest = rest - extra
    return np.array([bound] + counts)


def uneven(key, amount, total, limit, lean):
    if amount == 2:
        one = jax.random.randint(key, (), max(1, total - limit), min(limit, total - 1) + 1)
        return jnp.stack([one, total - one])
    sizes = jnp.asarray(length_profile(amount, total, limit, lean), jnp.int32)
    twos = (amount - 1) // 2
    source_of, taker = sizes[1:1 + 2 * twos:2], sizes[2:2 + 2 * twos:2]
    slack = jnp.minimum(source_of - 1, limit - taker)
    shifted = jax.random.randint(jax.random.fold_in(key, 1), (twos,), 0, 1 << 20) % (slack + 1)
    sizes = sizes.at[1:1 + 2 * twos:2].set(source_of - shifted).at[2:2 + 2 * twos:2].set(taker + shifted)
    return sizes[jax.random.permutation(jax.random.fold_in(key, 2), amount)]


def noise(key, shape, spread, reach, split=(), held_as=jnp.bfloat16):
    drawn = spread * jax.random.normal(key, shape, jnp.float32)
    if split:
        drawn = drawn * block_scale(key, shape, split, -0.22, 0.18)
    return jnp.clip(drawn, -reach, reach).astype(held_as)


def setup_inputs(seed: int = 0) -> dict:
    seeds = jax.random.split(jax.random.key(seed), 8)
    object_field = noise(seeds[0], (2, NH, NW), 0.5, 3.0, ((1, 8), (2, 4)), jnp.float32)
    probe_field = noise(seeds[1], (2, PW, PW), 1.0, 6.0, (), jnp.float32)
    amplitudes = jnp.clip(jnp.exp(math.log(16.0) - 3.465736 * jax.random.uniform(seeds[2], (N_ROW, N_COL, POOL, PW, PW), jnp.float32) ** block_scale(seeds[2], (N_ROW, N_COL, POOL, PW, PW), ((0, 8), (1, 4)), -0.2, 0.2)), 0.5, 16.0).astype(jnp.bfloat16)
    pos_rows = touch_ends(jax.random.randint(seeds[3], (N_ROW, N_COL, POOL), 0, TH), jax.random.fold_in(seeds[3], 1), 0, TH - 1).astype(jnp.int32)
    pos_cols = touch_ends(jax.random.randint(seeds[4], (N_ROW, N_COL, POOL), 0, TW), jax.random.fold_in(seeds[4], 1), 0, TW - 1).astype(jnp.int32)
    scan_pick = touch_ends(jax.random.randint(seeds[5], (N_ROW, N_COL, SCAP), 0, POOL), jax.random.fold_in(seeds[5], 1), 0, POOL - 1).astype(jnp.int32)
    scan_count = uneven(seeds[6], TILES, USED, SCAP, 2).astype(jnp.int32)
    return dict(object_field=object_field, probe_field=probe_field, amplitudes=amplitudes, pos_rows=pos_rows, pos_cols=pos_cols, scan_pick=scan_pick, scan_count=scan_count)


PRECISE = lax.Precision.HIGHEST
SOFTENING = 0.25
OBJECT_REG = 0.5
PROBE_REG = 1.0

def dft_tables(patch_width):
    grid_index = jnp.arange(patch_width, dtype=jnp.int32)
    phase_angle = (grid_index[:, None] * grid_index[None, :] % patch_width).astype(jnp.float32) * (2.0 * math.pi / patch_width)
    factor = 1.0 / math.sqrt(patch_width)
    return (jnp.cos(phase_angle) * factor, -jnp.sin(phase_angle) * factor)

def left_apply(table, data):
    return jnp.einsum('ka,sab->skb', table, data, precision=PRECISE)

def right_apply(data, table):
    return jnp.einsum('sab,bk->sak', data, table, precision=PRECISE)

def transform(real_part, imag_part, table_re, table_im):
    left_re = left_apply(table_re, real_part) - left_apply(table_im, imag_part)
    left_im = left_apply(table_re, imag_part) + left_apply(table_im, real_part)
    out_re = right_apply(left_re, table_re) - right_apply(left_im, table_im)
    out_im = right_apply(left_re, table_im) + right_apply(left_im, table_re)
    return (out_re, out_im)

def tile_terms(extended, probe_field, amps_tile, row_at, col_at, picks, count):
    patch_width = probe_field.shape[1]
    slot_count = picks.shape[0]
    table_re, table_im = dft_tables(patch_width)
    measured = amps_tile[picks].astype(jnp.float32)
    row_pick = row_at[picks].astype(jnp.int32)
    col_pick = col_at[picks].astype(jnp.int32)
    slot_live = (jnp.arange(slot_count, dtype=jnp.int32) < count).astype(jnp.float32)
    zero_idx = jnp.zeros((), jnp.int32)

    def cut_patch(row_start, col_start):
        return lax.dynamic_slice(extended, (zero_idx, row_start, col_start), (2, patch_width, patch_width))
    patches = jax.vmap(cut_patch)(row_pick, col_pick)
    object_re = patches[:, 0]
    object_im = patches[:, 1]
    probe_re = probe_field[0]
    probe_im = probe_field[1]
    wave_re = probe_re * object_re - probe_im * object_im
    wave_im = probe_re * object_im + probe_im * object_re
    far_re, far_im = transform(wave_re, wave_im, table_re, table_im)
    modulus = jnp.sqrt(far_re * far_re + far_im * far_im + SOFTENING)
    weight = (measured / modulus - 1.0) * slot_live[:, None, None]
    back_re, back_im = transform(far_re * weight, far_im * weight, table_re, -table_im)
    grad_re = probe_re * back_re + probe_im * back_im
    grad_im = probe_re * back_im - probe_im * back_re
    probe_grad_re = lax.optimization_barrier(jnp.sum(object_re * back_re + object_im * back_im, axis=0))
    probe_grad_im = lax.optimization_barrier(jnp.sum(object_re * back_im - object_im * back_re, axis=0))
    probe_light = lax.optimization_barrier(jnp.sum(slot_live[:, None, None] * (object_re * object_re + object_im * object_im), axis=0))
    lamp_power = probe_re * probe_re + probe_im * probe_im
    pieces = jnp.stack([grad_re, grad_im, slot_live[:, None, None] * lamp_power[None]], axis=1)
    grad_ext = jnp.zeros((3,) + extended.shape[1:], jnp.float32)

    def place_patch(slot_idx, running_sum):
        corner_at = (zero_idx, row_pick[slot_idx], col_pick[slot_idx])
        current = lax.dynamic_slice(running_sum, corner_at, (3, patch_width, patch_width))
        return lax.dynamic_update_slice(running_sum, current + pieces[slot_idx], corner_at)
    grad_ext = lax.fori_loop(0, slot_count, place_patch, grad_ext)
    return (grad_ext, (probe_grad_re, probe_grad_im, probe_light))

def reference(object_field, probe_field, amplitudes, pos_rows, pos_cols, scan_pick, scan_count):
    rim_width = PW // 2
    padded = jnp.pad(object_field, ((0, 0), (rim_width, rim_width), (rim_width, rim_width)))
    grad_all = jnp.zeros((3, NH + 2 * rim_width, NW + 2 * rim_width), jnp.float32)
    zero_plane = jnp.zeros((PW, PW), jnp.float32)
    zero_idx = jnp.zeros((), jnp.int32)

    def per_tile(tile_idx, carry):
        grad_now, sums_now = carry
        tile_pos = jnp.asarray(tile_idx).astype(jnp.int32)
        tile_row = tile_pos // N_COL
        tile_col = tile_pos % N_COL
        corner_at = (zero_idx, (tile_row * TH).astype(jnp.int32), (tile_col * TW).astype(jnp.int32))
        extended = lax.dynamic_slice(padded, corner_at, (2, TH + 2 * rim_width, TW + 2 * rim_width))
        grad_ext, probe_terms = tile_terms(extended, probe_field, amplitudes[tile_row, tile_col], pos_rows[tile_row, tile_col], pos_cols[tile_row, tile_col], scan_pick[tile_row, tile_col], scan_count[tile_pos])
        current = lax.dynamic_slice(grad_now, corner_at, (3, TH + 2 * rim_width, TW + 2 * rim_width))
        grad_now = lax.dynamic_update_slice(grad_now, current + grad_ext, corner_at)
        sums_now = (sums_now[0] + probe_terms[0], sums_now[1] + probe_terms[1], sums_now[2] + probe_terms[2])
        return (grad_now, sums_now)
    grad_all, probe_sums = lax.fori_loop(0, N_ROW * N_COL, per_tile, (grad_all, (zero_plane, zero_plane, zero_plane)))
    inside = grad_all[:, rim_width:rim_width + NH, rim_width:rim_width + NW]
    object_next = object_field + inside[0:2] / (inside[2] + OBJECT_REG)
    probe_next = probe_field + jnp.stack([probe_sums[0], probe_sums[1]]) / (probe_sums[2] + PROBE_REG)
    return (object_next, probe_next)
```

```python
import functools
import math

import jax
import jax.numpy as jnp
import ml_dtypes
import numpy as np
from jax import lax
from jax.experimental import pallas as pl
from jax.experimental.pallas import tpu as pltpu
from jax.sharding import PartitionSpec as P

SOFTENING = 0.25
OBJECT_REG = 0.5
PROBE_REG = 1.0
MESH = pl.DeviceIdType.MESH
VMEM_BYTES = 48 * 1024 * 1024
SUB = 8
WAYS = [(-1, 0), (1, 0), (0, -1), (0, 1), (-1, -1), (-1, 1), (1, -1), (1, 1)]
F32 = jnp.float32


def place(mesh_shape):
    return (lax.axis_index("row"), lax.axis_index("col"))


def exists(at, way, sizes, sign):
    conds = []
    for pos, step, size in zip(at, way, sizes):
        if step * sign == 1:
            conds.append(pos < size - 1)
        elif step * sign == -1:
            conds.append(pos > 0)
    return functools.reduce(jnp.logical_and, conds)


def greet(barrier, at, sizes, extra):
    total = jnp.int32(len(extra))
    for way in WAYS:
        here = exists(at, way, sizes, 1)

        @pl.when(here)
        def _(way=way):
            pl.semaphore_signal(
                barrier, inc=1, device_id=(at[0] + way[0], at[1] + way[1]), device_id_type=MESH
            )

        total = total + here.astype(jnp.int32)
    for peer in extra:
        pl.semaphore_signal(barrier, inc=1, device_id=peer, device_id_type=MESH)
    pl.semaphore_wait(barrier, total)


def halo_kernel(sizes, rim, obj, ext, send_sem, recv_sem, own_sem):
    high, wide = obj.shape[1:]
    at = place(sizes)
    greet(pltpu.get_barrier_semaphore(), at, sizes, [])
    src = {-1: lambda n: (0, rim), 0: lambda n: (0, n), 1: lambda n: (n - rim, rim)}
    dst = {-1: lambda n: (rim + n, rim), 0: lambda n: (rim, n), 1: lambda n: (0, rim)}

    def cut(ref, table, way):
        r, c = table[way[0]](high), table[way[1]](wide)
        return ref.at[:, pl.ds(*r), pl.ds(*c)]

    copies = [
        pltpu.make_async_remote_copy(
            src_ref=cut(obj, src, way),
            dst_ref=cut(ext, dst, way),
            send_sem=send_sem.at[k],
            recv_sem=recv_sem.at[k],
            device_id=(at[0] + way[0], at[1] + way[1]),
            device_id_type=MESH,
        )
        for k, way in enumerate(WAYS)
    ]
    for copy, way in zip(copies, WAYS):
        pl.when(exists(at, way, sizes, 1))(copy.start)
    own = pltpu.make_async_copy(obj, ext.at[:, pl.ds(rim, high), pl.ds(rim, wide)], own_sem)
    own.start()
    for way in WAYS:

        @pl.when(jnp.logical_not(exists(at, way, sizes, -1)))
        def _(way=way):
            (r, nr), (c, nc) = dst[way[0]](high), dst[way[1]](wide)
            ext[:, r : r + nr, c : c + nc] = jnp.zeros((2, nr, nc), F32)

    own.wait()
    for copy, way in zip(copies, WAYS):
        pl.when(exists(at, way, sizes, 1))(copy.wait_send)
        pl.when(exists(at, way, sizes, -1))(copy.wait_recv)


def split(x):
    hi = x.astype(jnp.bfloat16)
    return hi, (x - hi.astype(F32)).astype(jnp.bfloat16)


def dot(a, b):
    return jnp.dot(a, b, preferred_element_type=F32)


def left(table_hi, table_lo, x):
    hi, lo = split(x)
    return dot(table_hi[...], hi) + (dot(table_hi[...], lo) + dot(table_lo[...], hi))


def right(x, table_hi, table_lo):
    hi, lo = split(x)
    return dot(hi, table_hi[...]) + (dot(lo, table_hi[...]) + dot(hi, table_lo[...]))


def work_kernel(
    rows, cols, picks, count, ext, probe, amps, m_hi, m_lo, n_hi, n_lo, grad, sums, obj, wave
):
    width = probe.shape[1]
    slots = picks.shape[0]
    span = ext.shape[2]
    for s in range(slots):
        r, c = rows[picks[s]], cols[picks[s]]
        for p in range(2):
            base = pl.multiple_of(r // SUB * SUB, SUB)
            tall = width + SUB
            band = pltpu.roll(ext[p, pl.ds(base, tall), :], lax.rem(span - c, span), 1)[:, :width]
            obj[s, p] = pltpu.roll(band, lax.rem(tall - r % SUB, tall), 0)[:width]
    pr, pi = probe[0], probe[1]
    for s in range(slots):
        here = slice(s * width, (s + 1) * width)
        wave[:width, here] = pr * obj[s, 0] - pi * obj[s, 1]
        wave[width:, here] = pr * obj[s, 1] + pi * obj[s, 0]

    def turn(x):
        return jnp.concatenate(
            [
                jnp.concatenate(
                    [x[:width, s * width : (s + 1) * width], x[width:, s * width : (s + 1) * width]],
                    axis=1,
                )
                for s in range(slots)
            ],
            axis=0,
        )

    far = right(turn(left(m_hi, m_lo, wave[...])), n_hi, n_lo)
    for s in range(slots):
        here = slice(s * width, (s + 1) * width)
        live = (count[0] > s).astype(F32)
        fr, fi = far[here, :width], far[here, width:]
        measured = amps[picks[s]].astype(F32)
        weight = (measured * lax.rsqrt(fr * fr + fi * fi + SOFTENING) - 1.0) * live
        wave[:width, here] = fr * weight
        wave[width:, here] = fi * weight
    back = right(turn(left(n_hi, n_lo, wave[...])), m_hi, m_lo)
    grad[...] = jnp.zeros(grad.shape, F32)
    lamp = pr * pr + pi * pi
    totals = [jnp.zeros((width, width), F32)] * 3
    for s in range(slots):
        here = slice(s * width, (s + 1) * width)
        live = (count[0] > s).astype(F32)
        br, bi = back[here, :width], back[here, width:]
        o_r, o_i = obj[s, 0], obj[s, 1]
        totals[0] = totals[0] + (o_r * br + o_i * bi)
        totals[1] = totals[1] + (o_r * bi - o_i * br)
        totals[2] = totals[2] + live * (o_r * o_r + o_i * o_i)
        r, c = rows[picks[s]], cols[picks[s]]
        pieces = (pr * br + pi * bi, pr * bi - pi * br, live * lamp)
        for p, piece in enumerate(pieces):
            base = pl.multiple_of(r // SUB * SUB, SUB)
            piece = jnp.concatenate([piece, jnp.zeros((SUB, width), F32)], axis=0)
            piece = pltpu.roll(piece, r % SUB, 0)
            piece = jnp.concatenate([piece, jnp.zeros((width + SUB, span - width), F32)], axis=1)
            grad[p, pl.ds(base, width + SUB), :] += pltpu.roll(piece, c, 1)
    for p in range(3):
        sums[p] = totals[p].reshape(width // SUB, SUB, width)


def stages(sizes):
    out = []
    for axis in (1, 0):
        stride, rest = 1, sizes[axis]
        while rest > 1:
            p = next(f for f in range(2, rest + 1) if rest % f == 0)
            out.append((axis, stride, p))
            stride, rest = stride * p, rest // p
    return out


def fold_kernel(sizes, rim, steps, n_in, *refs):
    grad, sums, obj, probe, obj_out, probe_out, acc, cen = refs[:8]
    bufs = refs[8 : 8 + len(WAYS)]
    stage_bufs = refs[8 + len(WAYS) : 8 + len(WAYS) + len(steps)]
    send_sem, recv_sem, rs_send, rs_recv, ag_send, ag_recv = refs[8 + len(WAYS) + len(steps) :]
    high, wide = obj.shape[1:]
    at = place(sizes)

    def peer(step, k):
        axis, stride, p, _, _ = step
        digit = lax.rem(at[axis] // stride, p)
        other = lax.rem(digit + k, p)
        index = at[axis] + (other - digit) * stride
        return ((index, at[1]) if axis == 0 else (at[0], index)), digit, other

    everyone = [peer(step, k)[0] for step in steps for k in range(1, step[2])]
    greet(pltpu.get_barrier_semaphore(), at, sizes, everyone)

    src = {-1: lambda n: (0, rim), 0: lambda n: (rim, n), 1: lambda n: (rim + n, rim)}
    dst = {-1: lambda n: (n - rim, rim), 0: lambda n: (0, n), 1: lambda n: (0, rim)}
    copies = []
    for k, way in enumerate(WAYS):
        r, c = src[way[0]](high), src[way[1]](wide)
        copies.append(
            pltpu.make_async_remote_copy(
                src_ref=grad.at[:, pl.ds(*r), pl.ds(*c)],
                dst_ref=bufs[k],
                send_sem=send_sem.at[k],
                recv_sem=recv_sem.at[k],
                device_id=(at[0] + way[0], at[1] + way[1]),
                device_id_type=MESH,
            )
        )

    def begin_halo():
        for copy, way in zip(copies, WAYS):
            pl.when(exists(at, way, sizes, 1))(copy.start)

    acc[...] = sums[...]
    units = sums.shape[1]
    off = jnp.int32(0)
    pending = []
    undo = []
    sem = 0
    for i, step in enumerate(steps):
        axis, stride, p, size, scatter = step
        part = size // p if scatter else size
        moved = []
        for k in range(1, p):
            device, digit, other = peer(step, k)
            start = off + other * part if scatter else off
            copy = pltpu.make_async_remote_copy(
                src_ref=acc.at[:, pl.ds(start, part)],
                dst_ref=stage_bufs[i].at[k],
                send_sem=rs_send.at[sem],
                recv_sem=rs_recv.at[sem],
                device_id=device,
                device_id_type=MESH,
            )
            copy.start()
            moved.append(copy)
            sem += 1
        if i == 0:
            begin_halo()
        digit = peer(step, 1)[1]
        for copy in moved:
            copy.wait_recv()
        if scatter:
            undo.append((step, off, part))
            off = off + digit * part
            pending += moved
            total = acc[:, pl.ds(off, part)]
            for k in range(1, p):
                total = total + stage_bufs[i][k]
            acc[:, pl.ds(off, part)] = total
        else:
            for copy in moved:
                copy.wait_send()
            stage_bufs[i][0] = acc[:, pl.ds(off, part)]
            total = jnp.zeros((3, part) + acc.shape[2:], F32)
            for j in range(p):
                total = total + stage_bufs[i][lax.rem(digit - j + p, p)]
            acc[:, pl.ds(off, part)] = total
    part = steps[-1][3] // steps[-1][2] if steps[-1][4] else steps[-1][3]
    reg = acc[2, pl.ds(off, part)] + PROBE_REG
    for p in range(2):
        probe_out[p, pl.ds(off, part)] = probe[p, pl.ds(off, part)] + acc[p, pl.ds(off, part)] / reg

    def finish_object():
        cen[...] = grad[:, rim : rim + high, rim : rim + wide]
        for k, (copy, way) in enumerate(zip(copies, WAYS)):

            @pl.when(exists(at, way, sizes, -1))
            def _(k=k, copy=copy, way=way):
                copy.wait_recv()
                (r, nr), (c, nc) = dst[way[0]](high), dst[way[1]](wide)
                cen[:, r : r + nr, c : c + nc] += bufs[k][...]

        light = cen[2] + OBJECT_REG
        for p in range(2):
            obj_out[p] = obj[p] + cen[p] / light

    sem = 0
    for n, (step, base, part) in enumerate(reversed(undo)):
        p = step[2]
        moved = []
        for k in range(1, p):
            device, digit, other = peer(step, k)
            here = probe_out.at[:, pl.ds(base + digit * part, part)]
            copy = pltpu.make_async_remote_copy(
                src_ref=here,
                dst_ref=here,
                send_sem=ag_send.at[sem],
                recv_sem=ag_recv.at[sem],
                device_id=device,
                device_id_type=MESH,
            )
            copy.start()
            moved.append(copy)
            sem += 1
        for copy in moved:
            copy.wait_recv()
        pending += moved
    finish_object()
    for copy in pending:
        copy.wait_send()
    for copy, way in zip(copies, WAYS):
        pl.when(exists(at, way, sizes, 1))(copy.wait_send)


def tables(width):
    grid = np.arange(width)
    angle = (grid[:, None] * grid[None, :] % width) * (2.0 * math.pi / width)
    cos, sin = np.cos(angle) / math.sqrt(width), -np.sin(angle) / math.sqrt(width)
    out = []
    for full in (np.block([[cos, -sin], [sin, cos]]), np.block([[cos, sin], [-sin, cos]])):
        full = full.astype(np.float32)
        hi = full.astype(ml_dtypes.bfloat16)
        out += [hi, (full - hi.astype(np.float32)).astype(ml_dtypes.bfloat16)]
    return out


def per_device(
    sizes, object_field, probe_field, amplitudes, pos_rows, pos_cols, scan_pick, scan_count
):
    _, high, wide = object_field.shape
    width = probe_field.shape[1]
    rim = width // 2
    slots = scan_pick.shape[2]
    vmem = pl.BlockSpec(memory_space=pltpu.VMEM)
    smem = pl.BlockSpec(memory_space=pltpu.SMEM)
    dma = pltpu.SemaphoreType.DMA
    outer = (high + 2 * rim, wide + 2 * rim)
    ext = pl.pallas_call(
        functools.partial(halo_kernel, sizes, rim),
        out_shape=jax.ShapeDtypeStruct((2,) + outer, F32),
        in_specs=[vmem],
        out_specs=vmem,
        scratch_shapes=[dma((len(WAYS),)), dma((len(WAYS),)), dma],
        compiler_params=pltpu.CompilerParams(
            collective_id=0, has_side_effects=True, vmem_limit_bytes=VMEM_BYTES
        ),
        name="object_halo",
    )(object_field)
    grad, sums = pl.pallas_call(
        work_kernel,
        out_shape=[
            jax.ShapeDtypeStruct((3,) + outer, F32),
            jax.ShapeDtypeStruct((3, width // SUB, SUB, width), F32),
        ],
        in_specs=[smem] * 4 + [vmem] * 7,
        out_specs=[vmem, vmem],
        scratch_shapes=[
            pltpu.VMEM((slots, 2, width, width), F32),
            pltpu.VMEM((2 * width, slots * width), F32),
        ],
        compiler_params=pltpu.CompilerParams(vmem_limit_bytes=VMEM_BYTES),
        name="scan_terms",
    )(
        pos_rows[0, 0],
        pos_cols[0, 0],
        scan_pick[0, 0],
        scan_count,
        ext,
        probe_field,
        amplitudes[0, 0],
        *tables(width),
    )
    size = width // SUB
    steps = []
    for axis, stride, p in stages(sizes):
        scatter = size % p == 0
        steps.append((axis, stride, p, size, scatter))
        size = size // p if scatter else size
    sems = sum(step[2] - 1 for step in steps)
    lengths = {-1: lambda n: rim, 0: lambda n: n, 1: lambda n: rim}
    object_next, probe_next = pl.pallas_call(
        functools.partial(fold_kernel, sizes, rim, steps, 4),
        out_shape=[
            jax.ShapeDtypeStruct(object_field.shape, F32),
            jax.ShapeDtypeStruct((2, width // SUB, SUB, width), F32),
        ],
        in_specs=[vmem] * 4,
        out_specs=[vmem, vmem],
        scratch_shapes=[
            pltpu.VMEM((3, width // SUB, SUB, width), F32),
            pltpu.VMEM((3, high, wide), F32),
        ]
        + [pltpu.VMEM((3, lengths[r](high), lengths[c](wide)), F32) for r, c in WAYS]
        + [
            pltpu.VMEM((p, 3, size // p if scatter else size, SUB, width), F32)
            for _, _, p, size, scatter in steps
        ]
        + [dma((len(WAYS),)), dma((len(WAYS),))]
        + [dma((sems,))] * 4,
        compiler_params=pltpu.CompilerParams(
            collective_id=1, has_side_effects=True, vmem_limit_bytes=VMEM_BYTES
        ),
        name="fold",
    )(grad, sums, object_field, probe_field.reshape(2, width // SUB, SUB, width))
    return object_next, probe_next.reshape(probe_field.shape)


def solution(mesh):
    sizes = (mesh.shape["row"], mesh.shape["col"])
    in_specs = (
        P(None, "row", "col"),
        P(),
        P("row", "col", None, None, None),
        P("row", "col", None),
        P("row", "col", None),
        P("row", "col", None),
        P(("row", "col")),
    )
    out_specs = (P(None, "row", "col"), P())
    return jax.shard_map(
        functools.partial(per_device, sizes),
        mesh=mesh,
        in_specs=in_specs,
        out_specs=out_specs,
        check_vma=False,
    )
```

```python
import functools
import math

import jax
import jax.numpy as jnp
import ml_dtypes
import numpy as np
from jax import lax
from jax.experimental import pallas as pl
from jax.experimental.pallas import tpu as pltpu
from jax.sharding import PartitionSpec as P

SOFTENING = 0.25
OBJECT_REG = 0.5
PROBE_REG = 1.0
MESH = pl.DeviceIdType.MESH
VMEM_BYTES = 48 * 1024 * 1024
SUB = 8
WAYS = [(-1, 0), (1, 0), (0, -1), (0, 1)]
F32 = jnp.float32


def place(mesh_shape):
    return (lax.axis_index("row"), lax.axis_index("col"))


def exists(at, way, sizes, sign):
    conds = []
    for pos, step, size in zip(at, way, sizes):
        if step * sign == 1:
            conds.append(pos < size - 1)
        elif step * sign == -1:
            conds.append(pos > 0)
    return functools.reduce(jnp.logical_and, conds)


def greet(barrier, at, sizes, extra):
    total = jnp.int32(len(extra))
    for way in WAYS:
        here = exists(at, way, sizes, 1)

        @pl.when(here)
        def _(way=way):
            pl.semaphore_signal(
                barrier, inc=1, device_id=(at[0] + way[0], at[1] + way[1]), device_id_type=MESH
            )

        total = total + here.astype(jnp.int32)
    for peer in extra:
        pl.semaphore_signal(barrier, inc=1, device_id=peer, device_id_type=MESH)
    pl.semaphore_wait(barrier, total)


def halo_kernel(sizes, rim, obj, ext, send_sem, recv_sem, own_sem):
    high, wide = obj.shape[1:]
    at = place(sizes)
    greet(pltpu.get_barrier_semaphore(), at, sizes, [])
    src = {-1: lambda n: (0, rim), 0: lambda n: (0, n), 1: lambda n: (n - rim, rim)}
    dst = {-1: lambda n: (rim + n, rim), 0: lambda n: (rim, n), 1: lambda n: (0, rim)}

    def ends(way):
        if way[0]:
            inner = pl.ds(rim, wide)
            return (
                obj.at[:, pl.ds(*src[way[0]](high)), :],
                ext.at[:, pl.ds(*dst[way[0]](high)), inner],
            )
        start, size = src[way[1]](wide)
        return (
            ext.at[:, :, pl.ds(start + rim, size)],
            ext.at[:, :, pl.ds(*dst[way[1]](wide))],
        )

    copies = [
        pltpu.make_async_remote_copy(
            src_ref=ends(way)[0],
            dst_ref=ends(way)[1],
            send_sem=send_sem.at[k],
            recv_sem=recv_sem.at[k],
            device_id=(at[0] + way[0], at[1] + way[1]),
            device_id_type=MESH,
        )
        for k, way in enumerate(WAYS)
    ]
    both = list(zip(copies, WAYS))
    for copy, way in both[:2]:
        pl.when(exists(at, way, sizes, 1))(copy.start)
    own = pltpu.make_async_copy(obj, ext.at[:, pl.ds(rim, high), pl.ds(rim, wide)], own_sem)
    own.start()
    for way in WAYS[:2]:

        @pl.when(jnp.logical_not(exists(at, way, sizes, -1)))
        def _(way=way):
            r, nr = dst[way[0]](high)
            ext[:, r : r + nr, rim : rim + wide] = jnp.zeros((2, nr, wide), F32)

    for way in WAYS[2:]:

        @pl.when(jnp.logical_not(exists(at, way, sizes, -1)))
        def _(way=way):
            c, nc = dst[way[1]](wide)
            ext[:, :, c : c + nc] = jnp.zeros((2, high + 2 * rim, nc), F32)

    own.wait()
    for copy, way in both[:2]:
        pl.when(exists(at, way, sizes, -1))(copy.wait_recv)
    for copy, way in both[2:]:
        pl.when(exists(at, way, sizes, 1))(copy.start)
    for copy, way in both[2:]:
        pl.when(exists(at, way, sizes, -1))(copy.wait_recv)
    for copy, way in both:
        pl.when(exists(at, way, sizes, 1))(copy.wait_send)


def split(x):
    hi = x.astype(jnp.bfloat16)
    return hi, (x - hi.astype(F32)).astype(jnp.bfloat16)


def dot(a, b):
    return jnp.dot(a, b, preferred_element_type=F32)


def left(table_hi, table_lo, x):
    hi, lo = split(x)
    return dot(table_hi[...], hi) + (dot(table_hi[...], lo) + dot(table_lo[...], hi))


def right(x, table_hi, table_lo):
    hi, lo = split(x)
    return dot(hi, table_hi[...]) + (dot(lo, table_hi[...]) + dot(hi, table_lo[...]))


def work_kernel(
    rows, cols, picks, count, ext, probe, *rest
):
    late, (grad, sums, obj, wave), held, sems = rest[:5], rest[5:9], rest[9:14], rest[14]
    loads = [pltpu.make_async_copy(a, b, sems.at[k]) for k, (a, b) in enumerate(zip(late, held))]
    for load in loads:
        load.start()
    amps, m_hi, m_lo, n_hi, n_lo = held
    width = probe.shape[1]
    slots = picks.shape[0]
    span = ext.shape[2]
    for s in range(slots):
        r, c = rows[picks[s]], cols[picks[s]]
        for p in range(2):
            base = pl.multiple_of(r // SUB * SUB, SUB)
            tall = width + SUB
            band = pltpu.roll(ext[p, pl.ds(base, tall), :], lax.rem(span - c, span), 1)[:, :width]
            obj[s, p] = pltpu.roll(band, lax.rem(tall - r % SUB, tall), 0)[:width]
    pr, pi = probe[0], probe[1]
    for s in range(slots):
        here = slice(s * width, (s + 1) * width)
        wave[:width, here] = pr * obj[s, 0] - pi * obj[s, 1]
        wave[width:, here] = pr * obj[s, 1] + pi * obj[s, 0]

    for load in loads:
        load.wait()

    def turn(x):
        return jnp.concatenate(
            [
                jnp.concatenate(
                    [x[:width, s * width : (s + 1) * width], x[width:, s * width : (s + 1) * width]],
                    axis=1,
                )
                for s in range(slots)
            ],
            axis=0,
        )

    far = right(turn(left(m_hi, m_lo, wave[...])), n_hi, n_lo)
    for s in range(slots):
        here = slice(s * width, (s + 1) * width)
        live = (count[0] > s).astype(F32)
        fr, fi = far[here, :width], far[here, width:]
        measured = amps[picks[s]].astype(F32)
        weight = (measured * lax.rsqrt(fr * fr + fi * fi + SOFTENING) - 1.0) * live
        wave[:width, here] = fr * weight
        wave[width:, here] = fi * weight
    back = right(turn(left(n_hi, n_lo, wave[...])), m_hi, m_lo)
    grad[...] = jnp.zeros(grad.shape, F32)
    lamp = pr * pr + pi * pi
    totals = [jnp.zeros((width, width), F32)] * 3
    for s in range(slots):
        here = slice(s * width, (s + 1) * width)
        live = (count[0] > s).astype(F32)
        br, bi = back[here, :width], back[here, width:]
        o_r, o_i = obj[s, 0], obj[s, 1]
        totals[0] = totals[0] + (o_r * br + o_i * bi)
        totals[1] = totals[1] + (o_r * bi - o_i * br)
        totals[2] = totals[2] + live * (o_r * o_r + o_i * o_i)
        r, c = rows[picks[s]], cols[picks[s]]
        pieces = (pr * br + pi * bi, pr * bi - pi * br, live * lamp)
        for p, piece in enumerate(pieces):
            base = pl.multiple_of(r // SUB * SUB, SUB)
            piece = jnp.concatenate([piece, jnp.zeros((SUB, width), F32)], axis=0)
            piece = pltpu.roll(piece, r % SUB, 0)
            piece = jnp.concatenate([piece, jnp.zeros((width + SUB, span - width), F32)], axis=1)
            grad[p, pl.ds(base, width + SUB), :] += pltpu.roll(piece, c, 1)
    for p in range(3):
        sums[p] = totals[p].reshape(width // SUB, SUB, width)


def stages(sizes):
    out = []
    for axis in (1, 0):
        stride, rest = 1, sizes[axis]
        while rest > 1:
            p = next(f for f in range(2, rest + 1) if rest % f == 0)
            out.append((axis, stride, p))
            stride, rest = stride * p, rest // p
    return out


def fold_kernel(sizes, rim, steps, n_in, *refs):
    grad, sums, obj, probe, obj_out, probe_out, acc, cen = refs[:8]
    bufs = refs[8 : 8 + len(WAYS)]
    stage_bufs = refs[8 + len(WAYS) : 8 + len(WAYS) + len(steps)]
    strips, send_sem, recv_sem, rs_send, rs_recv, ag_send, ag_recv = refs[
        8 + len(WAYS) + len(steps) :
    ]
    high, wide = obj.shape[1:]
    at = place(sizes)

    def peer(step, k):
        axis, stride, p, _, _ = step
        digit = lax.rem(at[axis] // stride, p)
        other = lax.rem(digit + k, p)
        index = at[axis] + (other - digit) * stride
        return ((index, at[1]) if axis == 0 else (at[0], index)), digit, other

    everyone = [peer(step, k)[0] for step in steps for k in range(1, step[2])]
    greet(pltpu.get_barrier_semaphore(), at, sizes, everyone)

    src = {-1: lambda n: (0, rim), 0: lambda n: (rim, n), 1: lambda n: (rim + n, rim)}
    dst = {-1: lambda n: (n - rim, rim), 0: lambda n: (0, n), 1: lambda n: (0, rim)}
    copies = []
    for k, way in enumerate(WAYS):
        copies.append(
            pltpu.make_async_remote_copy(
                src_ref=strips.at[k] if way[0] else grad.at[:, :, pl.ds(*src[way[1]](wide))],
                dst_ref=bufs[k],
                send_sem=send_sem.at[k],
                recv_sem=recv_sem.at[k],
                device_id=(at[0] + way[0], at[1] + way[1]),
                device_id_type=MESH,
            )
        )

    both = list(zip(copies, WAYS))

    def begin_cols():
        for copy, way in both[2:]:
            pl.when(exists(at, way, sizes, 1))(copy.start)

    def begin_rows():
        cen[...] = grad[:, rim : rim + high, rim : rim + wide]
        for k, way in enumerate(WAYS[:2]):
            r, nr = src[way[0]](high)
            strips[k] = grad[:, r : r + nr, rim : rim + wide]
        for j, (copy, side) in enumerate(both[2:], 2):

            @pl.when(exists(at, side, sizes, -1))
            def _(j=j, copy=copy, side=side):
                copy.wait_recv()
                c, nc = dst[side[1]](wide)
                cen[:, :, c : c + nc] += bufs[j][:, rim : rim + high, :]
                for k, way in enumerate(WAYS[:2]):
                    r, nr = src[way[0]](high)
                    strips[k, :, :, c : c + nc] += bufs[j][:, r : r + nr, :]

        for copy, way in both[:2]:
            pl.when(exists(at, way, sizes, 1))(copy.start)

    acc[...] = sums[...]
    units = sums.shape[1]
    off = jnp.int32(0)
    pending = []
    undo = []
    sem = 0
    for i, step in enumerate(steps):
        axis, stride, p, size, scatter = step
        part = size // p if scatter else size
        moved = []
        for k in range(1, p):
            device, digit, other = peer(step, k)
            start = off + other * part if scatter else off
            copy = pltpu.make_async_remote_copy(
                src_ref=acc.at[:, pl.ds(start, part)],
                dst_ref=stage_bufs[i].at[k],
                send_sem=rs_send.at[sem],
                recv_sem=rs_recv.at[sem],
                device_id=device,
                device_id_type=MESH,
            )
            copy.start()
            moved.append(copy)
            sem += 1
        if i == 0:
            begin_cols()
        if i == min(1, len(steps) - 1):
            begin_rows()
        digit = peer(step, 1)[1]
        for copy in moved:
            copy.wait_recv()
        if scatter:
            undo.append((step, off, part))
            off = off + digit * part
            pending += moved
            total = acc[:, pl.ds(off, part)]
            for k in range(1, p):
                total = total + stage_bufs[i][k]
            acc[:, pl.ds(off, part)] = total
        else:
            for copy in moved:
                copy.wait_send()
            stage_bufs[i][0] = acc[:, pl.ds(off, part)]
            total = jnp.zeros((3, part) + acc.shape[2:], F32)
            for j in range(p):
                total = total + stage_bufs[i][lax.rem(digit - j + p, p)]
            acc[:, pl.ds(off, part)] = total
    part = steps[-1][3] // steps[-1][2] if steps[-1][4] else steps[-1][3]
    reg = acc[2, pl.ds(off, part)] + PROBE_REG
    for p in range(2):
        probe_out[p, pl.ds(off, part)] = probe[p, pl.ds(off, part)] + acc[p, pl.ds(off, part)] / reg

    def finish_object():
        for k, (copy, way) in enumerate(both[:2]):

            @pl.when(exists(at, way, sizes, -1))
            def _(k=k, copy=copy, way=way):
                copy.wait_recv()
                r, nr = dst[way[0]](high)
                cen[:, r : r + nr, :] += bufs[k][...]

        light = cen[2] + OBJECT_REG
        for p in range(2):
            obj_out[p] = obj[p] + cen[p] / light

    sem = 0
    for n, (step, base, part) in enumerate(reversed(undo)):
        p = step[2]
        moved = []
        for k in range(1, p):
            device, digit, other = peer(step, k)
            here = probe_out.at[:, pl.ds(base + digit * part, part)]
            copy = pltpu.make_async_remote_copy(
                src_ref=here,
                dst_ref=here,
                send_sem=ag_send.at[sem],
                recv_sem=ag_recv.at[sem],
                device_id=device,
                device_id_type=MESH,
            )
            copy.start()
            moved.append(copy)
            sem += 1
        for copy in moved:
            copy.wait_recv()
        pending += moved
    finish_object()
    for copy in pending:
        copy.wait_send()
    for copy, way in zip(copies, WAYS):
        pl.when(exists(at, way, sizes, 1))(copy.wait_send)


def tables(width):
    grid = np.arange(width)
    angle = (grid[:, None] * grid[None, :] % width) * (2.0 * math.pi / width)
    cos, sin = np.cos(angle) / math.sqrt(width), -np.sin(angle) / math.sqrt(width)
    out = []
    for full in (np.block([[cos, -sin], [sin, cos]]), np.block([[cos, sin], [-sin, cos]])):
        full = full.astype(np.float32)
        hi = full.astype(ml_dtypes.bfloat16)
        out += [hi, (full - hi.astype(np.float32)).astype(ml_dtypes.bfloat16)]
    return out


def per_device(
    sizes, object_field, probe_field, amplitudes, pos_rows, pos_cols, scan_pick, scan_count
):
    _, high, wide = object_field.shape
    width = probe_field.shape[1]
    rim = width // 2
    slots = scan_pick.shape[2]
    vmem = pl.BlockSpec(memory_space=pltpu.VMEM)
    smem = pl.BlockSpec(memory_space=pltpu.SMEM)
    dma = pltpu.SemaphoreType.DMA
    outer = (high + 2 * rim, wide + 2 * rim)
    ext = pl.pallas_call(
        functools.partial(halo_kernel, sizes, rim),
        out_shape=jax.ShapeDtypeStruct((2,) + outer, F32),
        in_specs=[vmem],
        out_specs=vmem,
        scratch_shapes=[dma((len(WAYS),)), dma((len(WAYS),)), dma],
        compiler_params=pltpu.CompilerParams(
            collective_id=0, has_side_effects=True, vmem_limit_bytes=VMEM_BYTES
        ),
        name="object_halo",
    )(object_field)
    grad, sums = pl.pallas_call(
        work_kernel,
        out_shape=[
            jax.ShapeDtypeStruct((3,) + outer, F32),
            jax.ShapeDtypeStruct((3, width // SUB, SUB, width), F32),
        ],
        in_specs=[smem] * 4 + [vmem] * 2 + [pl.BlockSpec(memory_space=pl.ANY)] * 5,
        out_specs=[vmem, vmem],
        scratch_shapes=[
            pltpu.VMEM((slots, 2, width, width), F32),
            pltpu.VMEM((2 * width, slots * width), F32),
            pltpu.VMEM(amplitudes.shape[2:], jnp.bfloat16),
        ]
        + [pltpu.VMEM((2 * width, 2 * width), jnp.bfloat16)] * 4
        + [
            dma((5,)),
        ],
        compiler_params=pltpu.CompilerParams(vmem_limit_bytes=VMEM_BYTES),
        name="scan_terms",
    )(
        pos_rows[0, 0],
        pos_cols[0, 0],
        scan_pick[0, 0],
        scan_count,
        ext,
        probe_field,
        amplitudes[0, 0],
        *tables(width),
    )
    size = width // SUB
    steps = []
    for axis, stride, p in stages(sizes):
        scatter = size % p == 0
        steps.append((axis, stride, p, size, scatter))
        size = size // p if scatter else size
    sems = sum(step[2] - 1 for step in steps)
    object_next, probe_next = pl.pallas_call(
        functools.partial(fold_kernel, sizes, rim, steps, 4),
        out_shape=[
            jax.ShapeDtypeStruct(object_field.shape, F32),
            jax.ShapeDtypeStruct((2, width // SUB, SUB, width), F32),
        ],
        in_specs=[vmem] * 4,
        out_specs=[vmem, vmem],
        scratch_shapes=[
            pltpu.VMEM((3, width // SUB, SUB, width), F32),
            pltpu.VMEM((3, high, wide), F32),
        ]
        + [pltpu.VMEM((3, rim, wide) if r else (3, outer[0], rim), F32) for r, c in WAYS]
        + [
            pltpu.VMEM((p, 3, size // p if scatter else size, SUB, width), F32)
            for _, _, p, size, scatter in steps
        ]
        + [pltpu.VMEM((2, 3, rim, wide), F32)]
        + [dma((len(WAYS),)), dma((len(WAYS),))]
        + [dma((sems,))] * 4,
        compiler_params=pltpu.CompilerParams(
            collective_id=1, has_side_effects=True, vmem_limit_bytes=VMEM_BYTES
        ),
        name="fold",
    )(grad, sums, object_field, probe_field.reshape(2, width // SUB, SUB, width))
    return object_next, probe_next.reshape(probe_field.shape)


def solution(mesh):
    sizes = (mesh.shape["row"], mesh.shape["col"])
    in_specs = (
        P(None, "row", "col"),
        P(),
        P("row", "col", None, None, None),
        P("row", "col", None),
        P("row", "col", None),
        P("row", "col", None),
        P(("row", "col")),
    )
    out_specs = (P(None, "row", "col"), P())
    return jax.shard_map(
        functools.partial(per_device, sizes),
        mesh=mesh,
        in_specs=in_specs,
        out_specs=out_specs,
        check_vma=False,
    )
```

```python
import functools
import math

import jax
import jax.numpy as jnp
import ml_dtypes
import numpy as np
from jax import lax
from jax.experimental import pallas as pl
from jax.experimental.pallas import tpu as pltpu
from jax.sharding import PartitionSpec as P

SOFTENING = 0.25
OBJECT_REG = 0.5
PROBE_REG = 1.0
MESH = pl.DeviceIdType.MESH
VMEM_BYTES = 48 * 1024 * 1024
SUB = 8
WAYS = [(-1, 0), (1, 0), (0, -1), (0, 1)]
F32 = jnp.float32


def place(mesh_shape):
    return (lax.axis_index("row"), lax.axis_index("col"))


def exists(at, way, sizes, sign):
    conds = []
    for pos, step, size in zip(at, way, sizes):
        if step * sign == 1:
            conds.append(pos < size - 1)
        elif step * sign == -1:
            conds.append(pos > 0)
    return functools.reduce(jnp.logical_and, conds)


def greet(barrier, at, sizes, extra):
    total = jnp.int32(len(extra))
    for way in WAYS:
        here = exists(at, way, sizes, 1)

        @pl.when(here)
        def _(way=way):
            pl.semaphore_signal(
                barrier, inc=1, device_id=(at[0] + way[0], at[1] + way[1]), device_id_type=MESH
            )

        total = total + here.astype(jnp.int32)
    for peer in extra:
        pl.semaphore_signal(barrier, inc=1, device_id=peer, device_id_type=MESH)
    pl.semaphore_wait(barrier, total)


def halo_kernel(sizes, rim, obj, ext, send_sem, recv_sem, own_sem):
    high, wide = obj.shape[1:]
    at = place(sizes)
    greet(pltpu.get_barrier_semaphore(), at, sizes, [])
    src = {-1: lambda n: (0, rim), 0: lambda n: (0, n), 1: lambda n: (n - rim, rim)}
    dst = {-1: lambda n: (rim + n, rim), 0: lambda n: (rim, n), 1: lambda n: (0, rim)}

    def ends(way):
        if way[0]:
            inner = pl.ds(rim, wide)
            return (
                obj.at[:, pl.ds(*src[way[0]](high)), :],
                ext.at[:, pl.ds(*dst[way[0]](high)), inner],
            )
        start, size = src[way[1]](wide)
        return (
            ext.at[:, :, pl.ds(start + rim, size)],
            ext.at[:, :, pl.ds(*dst[way[1]](wide))],
        )

    copies = [
        pltpu.make_async_remote_copy(
            src_ref=ends(way)[0],
            dst_ref=ends(way)[1],
            send_sem=send_sem.at[k],
            recv_sem=recv_sem.at[k],
            device_id=(at[0] + way[0], at[1] + way[1]),
            device_id_type=MESH,
        )
        for k, way in enumerate(WAYS)
    ]
    both = list(zip(copies, WAYS))
    for copy, way in both[:2]:
        pl.when(exists(at, way, sizes, 1))(copy.start)
    own = pltpu.make_async_copy(obj, ext.at[:, pl.ds(rim, high), pl.ds(rim, wide)], own_sem)
    own.start()
    for way in WAYS[:2]:

        @pl.when(jnp.logical_not(exists(at, way, sizes, -1)))
        def _(way=way):
            r, nr = dst[way[0]](high)
            ext[:, r : r + nr, rim : rim + wide] = jnp.zeros((2, nr, wide), F32)

    for way in WAYS[2:]:

        @pl.when(jnp.logical_not(exists(at, way, sizes, -1)))
        def _(way=way):
            c, nc = dst[way[1]](wide)
            ext[:, :, c : c + nc] = jnp.zeros((2, high + 2 * rim, nc), F32)

    own.wait()
    for copy, way in both[:2]:
        pl.when(exists(at, way, sizes, -1))(copy.wait_recv)
    for copy, way in both[2:]:
        pl.when(exists(at, way, sizes, 1))(copy.start)
    for copy, way in both[2:]:
        pl.when(exists(at, way, sizes, -1))(copy.wait_recv)
    for copy, way in both:
        pl.when(exists(at, way, sizes, 1))(copy.wait_send)


def split(x):
    hi = x.astype(jnp.bfloat16)
    return hi, (x - hi.astype(F32)).astype(jnp.bfloat16)


def dot(a, b):
    return jnp.dot(a, b, preferred_element_type=F32)


def left(table_hi, table_lo, x):
    hi, lo = split(x)
    return dot(table_hi[...], hi) + (dot(table_hi[...], lo) + dot(table_lo[...], hi))


def right(x, table_hi, table_lo):
    hi, lo = split(x)
    return dot(hi, table_hi[...]) + (dot(lo, table_hi[...]) + dot(hi, table_lo[...]))


def work_kernel(
    rows, cols, picks, count, ext, probe, *rest
):
    late, (grad, sums, obj, wave), held, sems = rest[:2], rest[2:6], rest[6:8], rest[12]
    loads = [pltpu.make_async_copy(a, b, sems.at[k]) for k, (a, b) in enumerate(zip(late, held))]
    for load in loads:
        load.start()
    amps, half = held
    m_hi, m_lo, n_hi, n_lo = rest[8:12]
    width = probe.shape[1]
    slots = picks.shape[0]
    span = ext.shape[2]
    for s in range(slots):
        r, c = rows[picks[s]], cols[picks[s]]
        for p in range(2):
            base = pl.multiple_of(r // SUB * SUB, SUB)
            tall = width + SUB
            band = pltpu.roll(ext[p, pl.ds(base, tall), :], lax.rem(span - c, span), 1)[:, :width]
            obj[s, p] = pltpu.roll(band, lax.rem(tall - r % SUB, tall), 0)[:width]
    pr, pi = probe[0], probe[1]
    for s in range(slots):
        here = slice(s * width, (s + 1) * width)
        wave[:width, here] = pr * obj[s, 0] - pi * obj[s, 1]
        wave[width:, here] = pr * obj[s, 1] + pi * obj[s, 0]

    for load in loads:
        load.wait()
    one, two = slice(0, width), slice(width, 2 * width)
    for part, m, n in ((0, m_hi, n_hi), (1, m_lo, n_lo)):
        cos, sin = half[part, one], half[part, two]
        for t, up, down in ((m, -sin, sin), (n, sin, -sin)):
            t[one, one], t[one, two] = cos, up
            t[two, one], t[two, two] = down, cos

    def turn(x):
        return jnp.concatenate(
            [
                jnp.concatenate(
                    [x[:width, s * width : (s + 1) * width], x[width:, s * width : (s + 1) * width]],
                    axis=1,
                )
                for s in range(slots)
            ],
            axis=0,
        )

    far = right(turn(left(m_hi, m_lo, wave[...])), n_hi, n_lo)
    for s in range(slots):
        here = slice(s * width, (s + 1) * width)
        live = (count[0] > s).astype(F32)
        fr, fi = far[here, :width], far[here, width:]
        measured = amps[picks[s]].astype(F32)
        weight = (measured * lax.rsqrt(fr * fr + fi * fi + SOFTENING) - 1.0) * live
        wave[:width, here] = fr * weight
        wave[width:, here] = fi * weight
    back = right(turn(left(n_hi, n_lo, wave[...])), m_hi, m_lo)
    grad[...] = jnp.zeros(grad.shape, F32)
    lamp = pr * pr + pi * pi
    totals = [jnp.zeros((width, width), F32)] * 3
    for s in range(slots):
        here = slice(s * width, (s + 1) * width)
        live = (count[0] > s).astype(F32)
        br, bi = back[here, :width], back[here, width:]
        o_r, o_i = obj[s, 0], obj[s, 1]
        totals[0] = totals[0] + (o_r * br + o_i * bi)
        totals[1] = totals[1] + (o_r * bi - o_i * br)
        totals[2] = totals[2] + live * (o_r * o_r + o_i * o_i)
        r, c = rows[picks[s]], cols[picks[s]]
        pieces = (pr * br + pi * bi, pr * bi - pi * br, live * lamp)
        for p, piece in enumerate(pieces):
            base = pl.multiple_of(r // SUB * SUB, SUB)
            piece = jnp.concatenate([piece, jnp.zeros((SUB, width), F32)], axis=0)
            piece = pltpu.roll(piece, r % SUB, 0)
            piece = jnp.concatenate([piece, jnp.zeros((width + SUB, span - width), F32)], axis=1)
            grad[p, pl.ds(base, width + SUB), :] += pltpu.roll(piece, c, 1)
    for p in range(3):
        sums[p] = totals[p].reshape(width // SUB, SUB, width)


def stages(sizes):
    out = []
    for axis in (1, 0):
        stride, rest = 1, sizes[axis]
        while rest > 1:
            p = next(f for f in range(2, rest + 1) if rest % f == 0)
            out.append((axis, stride, p))
            stride, rest = stride * p, rest // p
    return out


def fold_kernel(sizes, rim, steps, n_in, *refs):
    grad, sums, obj, probe, obj_out, probe_out, acc, cen = refs[:8]
    bufs = refs[8 : 8 + len(WAYS)]
    stage_bufs = refs[8 + len(WAYS) : 8 + len(WAYS) + len(steps)]
    strips, send_sem, recv_sem, rs_send, rs_recv, ag_send, ag_recv = refs[
        8 + len(WAYS) + len(steps) :
    ]
    high, wide = obj.shape[1:]
    at = place(sizes)

    def peer(step, k):
        axis, stride, p, _, _ = step
        digit = lax.rem(at[axis] // stride, p)
        other = lax.rem(digit + k, p)
        index = at[axis] + (other - digit) * stride
        return ((index, at[1]) if axis == 0 else (at[0], index)), digit, other

    everyone = [peer(step, k)[0] for step in steps for k in range(1, step[2])]
    greet(pltpu.get_barrier_semaphore(), at, sizes, everyone)

    src = {-1: lambda n: (0, rim), 0: lambda n: (rim, n), 1: lambda n: (rim + n, rim)}
    dst = {-1: lambda n: (n - rim, rim), 0: lambda n: (0, n), 1: lambda n: (0, rim)}
    copies = []
    for k, way in enumerate(WAYS):
        copies.append(
            pltpu.make_async_remote_copy(
                src_ref=strips.at[k] if way[0] else grad.at[:, :, pl.ds(*src[way[1]](wide))],
                dst_ref=bufs[k],
                send_sem=send_sem.at[k],
                recv_sem=recv_sem.at[k],
                device_id=(at[0] + way[0], at[1] + way[1]),
                device_id_type=MESH,
            )
        )

    both = list(zip(copies, WAYS))

    def begin_cols():
        for copy, way in both[2:]:
            pl.when(exists(at, way, sizes, 1))(copy.start)

    def begin_rows():
        cen[...] = grad[:, rim : rim + high, rim : rim + wide]
        for k, way in enumerate(WAYS[:2]):
            r, nr = src[way[0]](high)
            strips[k] = grad[:, r : r + nr, rim : rim + wide]
        for j, (copy, side) in enumerate(both[2:], 2):

            @pl.when(exists(at, side, sizes, -1))
            def _(j=j, copy=copy, side=side):
                copy.wait_recv()
                c, nc = dst[side[1]](wide)
                cen[:, :, c : c + nc] += bufs[j][:, rim : rim + high, :]
                for k, way in enumerate(WAYS[:2]):
                    r, nr = src[way[0]](high)
                    strips[k, :, :, c : c + nc] += bufs[j][:, r : r + nr, :]

        for copy, way in both[:2]:
            pl.when(exists(at, way, sizes, 1))(copy.start)

    acc[...] = sums[...]
    units = sums.shape[1]
    off = jnp.int32(0)
    pending = []
    undo = []
    sem = 0
    for i, step in enumerate(steps):
        axis, stride, p, size, scatter = step
        part = size // p if scatter else size
        moved = []
        for k in range(1, p):
            device, digit, other = peer(step, k)
            start = off + other * part if scatter else off
            copy = pltpu.make_async_remote_copy(
                src_ref=acc.at[:, pl.ds(start, part)],
                dst_ref=stage_bufs[i].at[k],
                send_sem=rs_send.at[sem],
                recv_sem=rs_recv.at[sem],
                device_id=device,
                device_id_type=MESH,
            )
            copy.start()
            moved.append(copy)
            sem += 1
        if i == 0:
            begin_cols()
        if i == min(2, len(steps) - 1):
            begin_rows()
        digit = peer(step, 1)[1]
        for copy in moved:
            copy.wait_recv()
        if scatter:
            undo.append((step, off, part))
            off = off + digit * part
            pending += moved
            total = acc[:, pl.ds(off, part)]
            for k in range(1, p):
                total = total + stage_bufs[i][k]
            acc[:, pl.ds(off, part)] = total
        else:
            for copy in moved:
                copy.wait_send()
            stage_bufs[i][0] = acc[:, pl.ds(off, part)]
            total = jnp.zeros((3, part) + acc.shape[2:], F32)
            for j in range(p):
                total = total + stage_bufs[i][lax.rem(digit - j + p, p)]
            acc[:, pl.ds(off, part)] = total
    part = steps[-1][3] // steps[-1][2] if steps[-1][4] else steps[-1][3]
    reg = acc[2, pl.ds(off, part)] + PROBE_REG
    for p in range(2):
        probe_out[p, pl.ds(off, part)] = probe[p, pl.ds(off, part)] + acc[p, pl.ds(off, part)] / reg

    def finish_object():
        for k, (copy, way) in enumerate(both[:2]):

            @pl.when(exists(at, way, sizes, -1))
            def _(k=k, copy=copy, way=way):
                copy.wait_recv()
                r, nr = dst[way[0]](high)
                cen[:, r : r + nr, :] += bufs[k][...]

        light = cen[2] + OBJECT_REG
        for p in range(2):
            obj_out[p] = obj[p] + cen[p] / light

    sem = 0
    for n, (step, base, part) in enumerate(reversed(undo)):
        p = step[2]
        moved = []
        for k in range(1, p):
            device, digit, other = peer(step, k)
            here = probe_out.at[:, pl.ds(base + digit * part, part)]
            copy = pltpu.make_async_remote_copy(
                src_ref=here,
                dst_ref=here,
                send_sem=ag_send.at[sem],
                recv_sem=ag_recv.at[sem],
                device_id=device,
                device_id_type=MESH,
            )
            copy.start()
            moved.append(copy)
            sem += 1
        if n == max(0, len(undo) - 3):
            finish_object()
        for copy in moved:
            copy.wait_recv()
        pending += moved
    for copy in pending:
        copy.wait_send()
    for copy, way in zip(copies, WAYS):
        pl.when(exists(at, way, sizes, 1))(copy.wait_send)


def tables(width):
    grid = np.arange(width)
    angle = (grid[:, None] * grid[None, :] % width) * (2.0 * math.pi / width)
    cos, sin = np.cos(angle) / math.sqrt(width), -np.sin(angle) / math.sqrt(width)
    full = np.concatenate([cos, sin], axis=0).astype(np.float32)
    hi = full.astype(ml_dtypes.bfloat16)
    return np.stack([hi, (full - hi.astype(np.float32)).astype(ml_dtypes.bfloat16)])


def per_device(
    sizes, object_field, probe_field, amplitudes, pos_rows, pos_cols, scan_pick, scan_count
):
    _, high, wide = object_field.shape
    width = probe_field.shape[1]
    rim = width // 2
    slots = scan_pick.shape[2]
    vmem = pl.BlockSpec(memory_space=pltpu.VMEM)
    smem = pl.BlockSpec(memory_space=pltpu.SMEM)
    dma = pltpu.SemaphoreType.DMA
    outer = (high + 2 * rim, wide + 2 * rim)
    ext = pl.pallas_call(
        functools.partial(halo_kernel, sizes, rim),
        out_shape=jax.ShapeDtypeStruct((2,) + outer, F32),
        in_specs=[vmem],
        out_specs=vmem,
        scratch_shapes=[dma((len(WAYS),)), dma((len(WAYS),)), dma],
        compiler_params=pltpu.CompilerParams(
            collective_id=0, has_side_effects=True, vmem_limit_bytes=VMEM_BYTES
        ),
        name="object_halo",
    )(object_field)
    grad, sums = pl.pallas_call(
        work_kernel,
        out_shape=[
            jax.ShapeDtypeStruct((3,) + outer, F32),
            jax.ShapeDtypeStruct((3, width // SUB, SUB, width), F32),
        ],
        in_specs=[smem] * 4 + [vmem] * 2 + [pl.BlockSpec(memory_space=pl.ANY)] * 2,
        out_specs=[vmem, vmem],
        scratch_shapes=[
            pltpu.VMEM((slots, 2, width, width), F32),
            pltpu.VMEM((2 * width, slots * width), F32),
            pltpu.VMEM(amplitudes.shape[2:], jnp.bfloat16),
            pltpu.VMEM((2, 2 * width, width), jnp.bfloat16),
        ]
        + [pltpu.VMEM((2 * width, 2 * width), jnp.bfloat16)] * 4
        + [
            dma((2,)),
        ],
        compiler_params=pltpu.CompilerParams(vmem_limit_bytes=VMEM_BYTES),
        name="scan_terms",
    )(
        pos_rows[0, 0],
        pos_cols[0, 0],
        scan_pick[0, 0],
        scan_count,
        ext,
        probe_field,
        amplitudes[0, 0],
        tables(width),
    )
    size = width // SUB
    steps = []
    for axis, stride, p in stages(sizes):
        scatter = size % p == 0
        steps.append((axis, stride, p, size, scatter))
        size = size // p if scatter else size
    sems = sum(step[2] - 1 for step in steps)
    object_next, probe_next = pl.pallas_call(
        functools.partial(fold_kernel, sizes, rim, steps, 4),
        out_shape=[
            jax.ShapeDtypeStruct(object_field.shape, F32),
            jax.ShapeDtypeStruct((2, width // SUB, SUB, width), F32),
        ],
        in_specs=[vmem] * 4,
        out_specs=[vmem, vmem],
        scratch_shapes=[
            pltpu.VMEM((3, width // SUB, SUB, width), F32),
            pltpu.VMEM((3, high, wide), F32),
        ]
        + [pltpu.VMEM((3, rim, wide) if r else (3, outer[0], rim), F32) for r, c in WAYS]
        + [
            pltpu.VMEM((p, 3, size // p if scatter else size, SUB, width), F32)
            for _, _, p, size, scatter in steps
        ]
        + [pltpu.VMEM((2, 3, rim, wide), F32)]
        + [dma((len(WAYS),)), dma((len(WAYS),))]
        + [dma((sems,))] * 4,
        compiler_params=pltpu.CompilerParams(
            collective_id=1, has_side_effects=True, vmem_limit_bytes=VMEM_BYTES
        ),
        name="fold",
    )(grad, sums, object_field, probe_field.reshape(2, width // SUB, SUB, width))
    return object_next, probe_next.reshape(probe_field.shape)


def solution(mesh):
    sizes = (mesh.shape["row"], mesh.shape["col"])
    in_specs = (
        P(None, "row", "col"),
        P(),
        P("row", "col", None, None, None),
        P("row", "col", None),
        P("row", "col", None),
        P("row", "col", None),
        P(("row", "col")),
    )
    out_specs = (P(None, "row", "col"), P())
    return jax.shard_map(
        functools.partial(per_device, sizes),
        mesh=mesh,
        in_specs=in_specs,
        out_specs=out_specs,
        check_vma=False,
    )
```

```python
import functools
import math

import jax
import jax.numpy as jnp
import ml_dtypes
import numpy as np
from jax import lax
from jax.experimental import pallas as pl
from jax.experimental.pallas import tpu as pltpu
from jax.sharding import PartitionSpec as P

SOFTENING = 0.25
OBJECT_REG = 0.5
PROBE_REG = 1.0
MESH = pl.DeviceIdType.MESH
VMEM_BYTES = 48 * 1024 * 1024
SUB = 8
WAYS = [(-1, 0), (1, 0), (0, -1), (0, 1)]
F32 = jnp.float32


def place(mesh_shape):
    return (lax.axis_index("row"), lax.axis_index("col"))


def exists(at, way, sizes, sign):
    conds = []
    for pos, step, size in zip(at, way, sizes):
        if step * sign == 1:
            conds.append(pos < size - 1)
        elif step * sign == -1:
            conds.append(pos > 0)
    return functools.reduce(jnp.logical_and, conds)


def greet(barrier, at, sizes, extra):
    total = jnp.int32(len(extra))
    for way in WAYS:
        here = exists(at, way, sizes, 1)

        @pl.when(here)
        def _(way=way):
            pl.semaphore_signal(
                barrier, inc=1, device_id=(at[0] + way[0], at[1] + way[1]), device_id_type=MESH
            )

        total = total + here.astype(jnp.int32)
    for peer in extra:
        pl.semaphore_signal(barrier, inc=1, device_id=peer, device_id_type=MESH)
    pl.semaphore_wait(barrier, total)


def halo_kernel(sizes, rim, obj, ext, send_sem, recv_sem, own_sem):
    high, wide = obj.shape[1:]
    at = place(sizes)
    greet(pltpu.get_barrier_semaphore(), at, sizes, [])
    src = {-1: lambda n: (0, rim), 0: lambda n: (0, n), 1: lambda n: (n - rim, rim)}
    dst = {-1: lambda n: (rim + n, rim), 0: lambda n: (rim, n), 1: lambda n: (0, rim)}

    def ends(way):
        if way[0]:
            inner = pl.ds(rim, wide)
            return (
                obj.at[:, pl.ds(*src[way[0]](high)), :],
                ext.at[:, pl.ds(*dst[way[0]](high)), inner],
            )
        start, size = src[way[1]](wide)
        return (
            ext.at[:, :, pl.ds(start + rim, size)],
            ext.at[:, :, pl.ds(*dst[way[1]](wide))],
        )

    def send(ref, target, way, k):
        return pltpu.make_async_remote_copy(
            src_ref=ref,
            dst_ref=target,
            send_sem=send_sem.at[k],
            recv_sem=recv_sem.at[k],
            device_id=(at[0] + way[0], at[1] + way[1]),
            device_id_type=MESH,
        )

    both = [(send(*ends(way), way, k), way) for k, way in enumerate(WAYS[:2])]
    corners = []
    for way in WAYS[2:]:
        near, far = pl.ds(*src[way[1]](wide)), pl.ds(*dst[way[1]](wide))
        middle = send(obj.at[:, :, near], ext.at[:, pl.ds(rim, high), far], way, len(both))
        both.append((middle, way))
    for way in WAYS[2:]:
        whole, target = ends(way)
        for top in (0, rim + high):
            piece = pl.ds(top, rim)
            k = len(both) + len(corners)
            corners.append((send(whole.at[:, piece, :], target.at[:, piece, :], way, k), way))
    for copy, way in both:
        pl.when(exists(at, way, sizes, 1))(copy.start)
    own = pltpu.make_async_copy(obj, ext.at[:, pl.ds(rim, high), pl.ds(rim, wide)], own_sem)
    own.start()
    for way in WAYS[:2]:

        @pl.when(jnp.logical_not(exists(at, way, sizes, -1)))
        def _(way=way):
            r, nr = dst[way[0]](high)
            ext[:, r : r + nr, rim : rim + wide] = jnp.zeros((2, nr, wide), F32)

    for way in WAYS[2:]:

        @pl.when(jnp.logical_not(exists(at, way, sizes, -1)))
        def _(way=way):
            c, nc = dst[way[1]](wide)
            ext[:, :, c : c + nc] = jnp.zeros((2, high + 2 * rim, nc), F32)

    own.wait()
    for copy, way in both[:2]:
        pl.when(exists(at, way, sizes, -1))(copy.wait_recv)
    for copy, way in corners:
        pl.when(exists(at, way, sizes, 1))(copy.start)
    for copy, way in both[2:] + corners:
        pl.when(exists(at, way, sizes, -1))(copy.wait_recv)
    for copy, way in both + corners:
        pl.when(exists(at, way, sizes, 1))(copy.wait_send)


def split(x):
    hi = x.astype(jnp.bfloat16)
    return hi, (x - hi.astype(F32)).astype(jnp.bfloat16)


def dot(a, b):
    return jnp.dot(a, b, preferred_element_type=F32)


def left(table_hi, table_lo, x):
    hi, lo = split(x)
    return dot(table_hi[...], hi) + (dot(table_hi[...], lo) + dot(table_lo[...], hi))


def right(x, table_hi, table_lo):
    hi, lo = split(x)
    return dot(hi, table_hi[...]) + (dot(lo, table_hi[...]) + dot(hi, table_lo[...]))


def work_kernel(
    rows, cols, picks, count, ext, probe, *rest
):
    late, (grad, sums, obj, wave), held, sems = rest[:2], rest[2:6], rest[6:8], rest[12]
    loads = [pltpu.make_async_copy(a, b, sems.at[k]) for k, (a, b) in enumerate(zip(late, held))]
    for load in loads:
        load.start()
    amps, half = held
    m_hi, m_lo, n_hi, n_lo = rest[8:12]
    width = probe.shape[1]
    slots = picks.shape[0]
    span = ext.shape[2]
    for s in range(slots):
        r, c = rows[picks[s]], cols[picks[s]]
        for p in range(2):
            base = pl.multiple_of(r // SUB * SUB, SUB)
            tall = width + SUB
            band = pltpu.roll(ext[p, pl.ds(base, tall), :], lax.rem(span - c, span), 1)[:, :width]
            obj[s, p] = pltpu.roll(band, lax.rem(tall - r % SUB, tall), 0)[:width]
    pr, pi = probe[0], probe[1]
    for s in range(slots):
        here = slice(s * width, (s + 1) * width)
        wave[:width, here] = pr * obj[s, 0] - pi * obj[s, 1]
        wave[width:, here] = pr * obj[s, 1] + pi * obj[s, 0]

    for load in loads:
        load.wait()
    one, two = slice(0, width), slice(width, 2 * width)
    for part, m, n in ((0, m_hi, n_hi), (1, m_lo, n_lo)):
        cos, sin = half[part, one], half[part, two]
        for t, up, down in ((m, -sin, sin), (n, sin, -sin)):
            t[one, one], t[one, two] = cos, up
            t[two, one], t[two, two] = down, cos

    def turn(x):
        return jnp.concatenate(
            [
                jnp.concatenate(
                    [x[:width, s * width : (s + 1) * width], x[width:, s * width : (s + 1) * width]],
                    axis=1,
                )
                for s in range(slots)
            ],
            axis=0,
        )

    far = right(turn(left(m_hi, m_lo, wave[...])), n_hi, n_lo)
    for s in range(slots):
        here = slice(s * width, (s + 1) * width)
        live = (count[0] > s).astype(F32)
        fr, fi = far[here, :width], far[here, width:]
        measured = amps[picks[s]].astype(F32)
        weight = (measured * lax.rsqrt(fr * fr + fi * fi + SOFTENING) - 1.0) * live
        wave[:width, here] = fr * weight
        wave[width:, here] = fi * weight
    back = right(turn(left(n_hi, n_lo, wave[...])), m_hi, m_lo)
    grad[...] = jnp.zeros(grad.shape, F32)
    lamp = pr * pr + pi * pi
    totals = [jnp.zeros((width, width), F32)] * 3
    for s in range(slots):
        here = slice(s * width, (s + 1) * width)
        live = (count[0] > s).astype(F32)
        br, bi = back[here, :width], back[here, width:]
        o_r, o_i = obj[s, 0], obj[s, 1]
        totals[0] = totals[0] + (o_r * br + o_i * bi)
        totals[1] = totals[1] + (o_r * bi - o_i * br)
        totals[2] = totals[2] + live * (o_r * o_r + o_i * o_i)
        r, c = rows[picks[s]], cols[picks[s]]
        pieces = (pr * br + pi * bi, pr * bi - pi * br, live * lamp)
        for p, piece in enumerate(pieces):
            base = pl.multiple_of(r // SUB * SUB, SUB)
            piece = jnp.concatenate([piece, jnp.zeros((SUB, width), F32)], axis=0)
            piece = pltpu.roll(piece, r % SUB, 0)
            piece = jnp.concatenate([piece, jnp.zeros((width + SUB, span - width), F32)], axis=1)
            grad[p, pl.ds(base, width + SUB), :] += pltpu.roll(piece, c, 1)
    for p in range(3):
        sums[p] = totals[p].reshape(width // SUB, SUB, width)


def stages(sizes):
    out = []
    for axis in (1, 0):
        stride, rest = 1, sizes[axis]
        while rest > 1:
            p = next(f for f in range(2, rest + 1) if rest % f == 0)
            out.append((axis, stride, p))
            stride, rest = stride * p, rest // p
    return out


def fold_kernel(sizes, rim, steps, n_in, *refs):
    grad, sums, obj, probe, obj_out, probe_out, acc, cen = refs[:8]
    bufs = refs[8 : 8 + len(WAYS)]
    stage_bufs = refs[8 + len(WAYS) : 8 + len(WAYS) + len(steps)]
    strips, send_sem, recv_sem, rs_send, rs_recv, ag_send, ag_recv = refs[
        8 + len(WAYS) + len(steps) :
    ]
    high, wide = obj.shape[1:]
    at = place(sizes)

    def peer(step, k):
        axis, stride, p, _, _ = step
        digit = lax.rem(at[axis] // stride, p)
        other = lax.rem(digit + k, p)
        index = at[axis] + (other - digit) * stride
        return ((index, at[1]) if axis == 0 else (at[0], index)), digit, other

    everyone = [peer(step, k)[0] for step in steps for k in range(1, step[2])]
    greet(pltpu.get_barrier_semaphore(), at, sizes, everyone)

    src = {-1: lambda n: (0, rim), 0: lambda n: (rim, n), 1: lambda n: (rim + n, rim)}
    dst = {-1: lambda n: (n - rim, rim), 0: lambda n: (0, n), 1: lambda n: (0, rim)}
    copies = []
    for k, way in enumerate(WAYS):
        copies.append(
            pltpu.make_async_remote_copy(
                src_ref=strips.at[k] if way[0] else grad.at[:, :, pl.ds(*src[way[1]](wide))],
                dst_ref=bufs[k],
                send_sem=send_sem.at[k],
                recv_sem=recv_sem.at[k],
                device_id=(at[0] + way[0], at[1] + way[1]),
                device_id_type=MESH,
            )
        )

    both = list(zip(copies, WAYS))

    def begin_cols():
        for copy, way in both[2:]:
            pl.when(exists(at, way, sizes, 1))(copy.start)

    def begin_rows():
        cen[...] = grad[:, rim : rim + high, rim : rim + wide]
        for k, way in enumerate(WAYS[:2]):
            r, nr = src[way[0]](high)
            strips[k] = grad[:, r : r + nr, rim : rim + wide]
        for j, (copy, side) in enumerate(both[2:], 2):

            @pl.when(exists(at, side, sizes, -1))
            def _(j=j, copy=copy, side=side):
                copy.wait_recv()
                c, nc = dst[side[1]](wide)
                cen[:, :, c : c + nc] += bufs[j][:, rim : rim + high, :]
                for k, way in enumerate(WAYS[:2]):
                    r, nr = src[way[0]](high)
                    strips[k, :, :, c : c + nc] += bufs[j][:, r : r + nr, :]

        for copy, way in both[:2]:
            pl.when(exists(at, way, sizes, 1))(copy.start)

    acc[...] = sums[...]
    units = sums.shape[1]
    off = jnp.int32(0)
    pending = []
    undo = []
    sem = 0
    for i, step in enumerate(steps):
        axis, stride, p, size, scatter = step
        part = size // p if scatter else size
        moved = []
        for k in range(1, p):
            device, digit, other = peer(step, k)
            start = off + other * part if scatter else off
            copy = pltpu.make_async_remote_copy(
                src_ref=acc.at[:, pl.ds(start, part)],
                dst_ref=stage_bufs[i].at[k],
                send_sem=rs_send.at[sem],
                recv_sem=rs_recv.at[sem],
                device_id=device,
                device_id_type=MESH,
            )
            copy.start()
            moved.append(copy)
            sem += 1
        if i == 0:
            begin_cols()
        if i == min(2, len(steps) - 1):
            begin_rows()
        digit = peer(step, 1)[1]
        for copy in moved:
            copy.wait_recv()
        if scatter:
            undo.append((step, off, part))
            off = off + digit * part
            pending += moved
            total = acc[:, pl.ds(off, part)]
            for k in range(1, p):
                total = total + stage_bufs[i][k]
            acc[:, pl.ds(off, part)] = total
        else:
            for copy in moved:
                copy.wait_send()
            stage_bufs[i][0] = acc[:, pl.ds(off, part)]
            total = jnp.zeros((3, part) + acc.shape[2:], F32)
            for j in range(p):
                total = total + stage_bufs[i][lax.rem(digit - j + p, p)]
            acc[:, pl.ds(off, part)] = total
    part = steps[-1][3] // steps[-1][2] if steps[-1][4] else steps[-1][3]
    reg = acc[2, pl.ds(off, part)] + PROBE_REG
    for p in range(2):
        probe_out[p, pl.ds(off, part)] = probe[p, pl.ds(off, part)] + acc[p, pl.ds(off, part)] / reg

    def finish_object():
        for k, (copy, way) in enumerate(both[:2]):

            @pl.when(exists(at, way, sizes, -1))
            def _(k=k, copy=copy, way=way):
                copy.wait_recv()
                r, nr = dst[way[0]](high)
                cen[:, r : r + nr, :] += bufs[k][...]

        light = cen[2] + OBJECT_REG
        for p in range(2):
            obj_out[p] = obj[p] + cen[p] / light

    sem = 0
    for n, (step, base, part) in enumerate(reversed(undo)):
        p = step[2]
        moved = []
        for k in range(1, p):
            device, digit, other = peer(step, k)
            here = probe_out.at[:, pl.ds(base + digit * part, part)]
            copy = pltpu.make_async_remote_copy(
                src_ref=here,
                dst_ref=here,
                send_sem=ag_send.at[sem],
                recv_sem=ag_recv.at[sem],
                device_id=device,
                device_id_type=MESH,
            )
            copy.start()
            moved.append(copy)
            sem += 1
        if n == max(0, len(undo) - 3):
            finish_object()
        for copy in moved:
            copy.wait_recv()
        pending += moved
    for copy in pending:
        copy.wait_send()
    for copy, way in zip(copies, WAYS):
        pl.when(exists(at, way, sizes, 1))(copy.wait_send)


def tables(width):
    grid = np.arange(width)
    angle = (grid[:, None] * grid[None, :] % width) * (2.0 * math.pi / width)
    cos, sin = np.cos(angle) / math.sqrt(width), -np.sin(angle) / math.sqrt(width)
    full = np.concatenate([cos, sin], axis=0).astype(np.float32)
    hi = full.astype(ml_dtypes.bfloat16)
    return np.stack([hi, (full - hi.astype(np.float32)).astype(ml_dtypes.bfloat16)])


def per_device(
    sizes, object_field, probe_field, amplitudes, pos_rows, pos_cols, scan_pick, scan_count
):
    _, high, wide = object_field.shape
    width = probe_field.shape[1]
    rim = width // 2
    slots = scan_pick.shape[2]
    vmem = pl.BlockSpec(memory_space=pltpu.VMEM)
    smem = pl.BlockSpec(memory_space=pltpu.SMEM)
    dma = pltpu.SemaphoreType.DMA
    outer = (high + 2 * rim, wide + 2 * rim)
    ext = pl.pallas_call(
        functools.partial(halo_kernel, sizes, rim),
        out_shape=jax.ShapeDtypeStruct((2,) + outer, F32),
        in_specs=[vmem],
        out_specs=vmem,
        scratch_shapes=[dma((2 * len(WAYS),)), dma((2 * len(WAYS),)), dma],
        compiler_params=pltpu.CompilerParams(
            collective_id=0, has_side_effects=True, vmem_limit_bytes=VMEM_BYTES
        ),
        name="object_halo",
    )(object_field)
    grad, sums = pl.pallas_call(
        work_kernel,
        out_shape=[
            jax.ShapeDtypeStruct((3,) + outer, F32),
            jax.ShapeDtypeStruct((3, width // SUB, SUB, width), F32),
        ],
        in_specs=[smem] * 4 + [vmem] * 2 + [pl.BlockSpec(memory_space=pl.ANY)] * 2,
        out_specs=[vmem, vmem],
        scratch_shapes=[
            pltpu.VMEM((slots, 2, width, width), F32),
            pltpu.VMEM((2 * width, slots * width), F32),
            pltpu.VMEM(amplitudes.shape[2:], jnp.bfloat16),
            pltpu.VMEM((2, 2 * width, width), jnp.bfloat16),
        ]
        + [pltpu.VMEM((2 * width, 2 * width), jnp.bfloat16)] * 4
        + [
            dma((2,)),
        ],
        compiler_params=pltpu.CompilerParams(vmem_limit_bytes=VMEM_BYTES),
        name="scan_terms",
    )(
        pos_rows[0, 0],
        pos_cols[0, 0],
        scan_pick[0, 0],
        scan_count,
        ext,
        probe_field,
        amplitudes[0, 0],
        tables(width),
    )
    size = width // SUB
    steps = []
    for axis, stride, p in stages(sizes):
        scatter = size % p == 0
        steps.append((axis, stride, p, size, scatter))
        size = size // p if scatter else size
    sems = sum(step[2] - 1 for step in steps)
    object_next, probe_next = pl.pallas_call(
        functools.partial(fold_kernel, sizes, rim, steps, 4),
        out_shape=[
            jax.ShapeDtypeStruct(object_field.shape, F32),
            jax.ShapeDtypeStruct((2, width // SUB, SUB, width), F32),
        ],
        in_specs=[vmem] * 4,
        out_specs=[vmem, vmem],
        scratch_shapes=[
            pltpu.VMEM((3, width // SUB, SUB, width), F32),
            pltpu.VMEM((3, high, wide), F32),
        ]
        + [pltpu.VMEM((3, rim, wide) if r else (3, outer[0], rim), F32) for r, c in WAYS]
        + [
            pltpu.VMEM((p, 3, size // p if scatter else size, SUB, width), F32)
            for _, _, p, size, scatter in steps
        ]
        + [pltpu.VMEM((2, 3, rim, wide), F32)]
        + [dma((len(WAYS),)), dma((len(WAYS),))]
        + [dma((sems,))] * 4,
        compiler_params=pltpu.CompilerParams(
            collective_id=1, has_side_effects=True, vmem_limit_bytes=VMEM_BYTES
        ),
        name="fold",
    )(grad, sums, object_field, probe_field.reshape(2, width // SUB, SUB, width))
    return object_next, probe_next.reshape(probe_field.shape)


def solution(mesh):
    sizes = (mesh.shape["row"], mesh.shape["col"])
    in_specs = (
        P(None, "row", "col"),
        P(),
        P("row", "col", None, None, None),
        P("row", "col", None),
        P("row", "col", None),
        P("row", "col", None),
        P(("row", "col")),
    )
    out_specs = (P(None, "row", "col"), P())
    return jax.shard_map(
        functools.partial(per_device, sizes),
        mesh=mesh,
        in_specs=in_specs,
        out_specs=out_specs,
        check_vma=False,
    )
```
